32 devices in a mesh: replica: 2 (over y), dp: 4 (over x, core), tensor: 4 (over z).
Axes of the slice: x: 2, y: 2, z: 4, core: 2. Of those that a mesh axis runs over, the one named last changes fastest.
Arguments:
- hidden: bfloat16 [3, 1536, 8192], P(None, ('replica', 'dp'), 'tensor'), parts along dimension 1, may hold values from -6 to 6
- w_query: bfloat16 [8192, 4096], P(None, 'tensor'), may hold values from -0.0625 to 0.0625
- a_codes: bfloat16 [48, 8192, 128], P('dp', 'tensor'), may hold values from -0.0625 to 0.0625
- a_scales: float32 [48, 8192], P('dp', 'tensor'), may hold values from 0.5 to 2
- b_codes: bfloat16 [48, 128, 4096], P('dp', None, 'tensor'), may hold values from -0.5 to 0.5
- b_scales: float32 [48, 128], P('dp'), may hold values from 0.5 to 2
- variant_lists: int32 [8, 8], P('replica'), parts along dimension 0, may hold values from 0 to 47, as said below
- row_pick: int32 [1536], P(('replica', 'dp')), parts along dimension 0, may hold values from 0 to 7
- lengths: int32 [1536], P(('replica', 'dp', 'tensor')), parts along dimension 0, may hold values from 1 to 128, as said below
- page_table: int32 [1536, 8], P(('replica', 'dp', 'tensor')), parts along dimension 0, may hold values from 0 to 383, as said below
- new_kv: bfloat16 [3, 1536, 1024], P(None, ('replica', 'dp', 'tensor')), parts along dimension 1, may hold values from -6 to 6
- kv_cache: bfloat16 [12288, 16, 1024], P(('replica', 'dp', 'tensor')), parts along dimension 0
Outputs:
- attended: bfloat16 [3, 1536, 4096], P(None, ('replica', 'dp', 'tensor')), parts along dimension 1
The draws below stay inside these ranges and needn't reach their ends.
There are 2 independent parts, one for each index of `replica`. The reference program is written for one: setup_inputs(seed, part) draws one part's arguments, and reference() takes and returns one part's arrays. A program takes and returns all parts, laid end to end along the dimension named above; an argument that names none is the same for every part. Nothing has to cross between parts.
Inputs may be any that keep to these rules, and one draw needn't show every extreme that they name: `variant_lists`: in each group the 8 variants are distinct. Variant v is owned by block v // 12; no block holds more than 2 of one group's variants, and in every group some block holds exactly 2. `lengths`: some row has exactly 128 cached tokens. `page_table`: within each aligned block b of 48 rows the 384 entries are distinct and name the pages b * 384 + entry of the pool; entries past a row's length are not read.
All inputs are finite; a program needn't handle non-finite values.
Results may differ from the reference program's by a relative error of at most 0.015.
The reference program's roundings to bfloat16 on the way count: a program that leaves them out, or rounds other values in their place, can miss the bound.
Values may be sent and summed in bfloat16 or wider, within the bound.
A program may use at most 192 MiB of HBM per device.

```python
import math
import jax
import jax.numpy as jnp
from jax import lax

D = 8192
HEADS = 32
KVH = 4
HD = 128
RANK = 128
VARIANTS = 48
LIST = 8
SLOTS = 2
STEPS = 3
PAGE = 16
PAGES_ROW = 8
GROUP_ROWS = 192
GROUPS = 4
ROWS = 768
ROW_DEV = 48
OWNED = 12
CTX = 128
POOL_DEV = 384
POOL = 6144


def draw_variant_lists(key, part):
    key = jax.random.fold_in(key, 11)

    def one_group(group_key):
        owner_key, pick_key, rest_key, order_key = jax.random.split(group_key, 4)
        owner_order = jax.random.permutation(owner_key, GROUPS).astype(jnp.int32)
        pick_keys = jax.random.split(pick_key, GROUPS)

        def owner_picks(small_key):
            return jax.random.permutation(small_key, OWNED)[:SLOTS].astype(jnp.int32)
        picked = jax.vmap(owner_picks)(pick_keys)
        variant_grid = owner_order[:, None] * OWNED + picked[owner_order]
        leading = variant_grid[0]
        remaining = jax.random.permutation(rest_key, variant_grid[1:].reshape(-1))[:LIST - SLOTS]
        chosen_all = jnp.concatenate([leading, remaining.astype(jnp.int32)])
        return jax.random.permutation(order_key, chosen_all).astype(jnp.int32)
    return jax.vmap(one_group)(jax.random.split(key, GROUPS)).astype(jnp.int32)


def draw_lengths(key, part):
    key = jax.random.fold_in(key, 12)
    first_key, second_key = jax.random.split(key)
    drawn = jax.random.randint(first_key, (ROWS,), 1, CTX + 1).astype(jnp.int32)
    longest = jax.random.randint(second_key, (), 0, ROWS).astype(jnp.int32)
    return jnp.where(jnp.arange(ROWS, dtype=jnp.int32) == longest, CTX, drawn).astype(jnp.int32)


def draw_page_table(key, part):
    key = jax.random.fold_in(key, 13)

    def one_block(block_key):
        return jax.random.permutation(block_key, POOL_DEV).astype(jnp.int32).reshape(ROW_DEV, PAGES_ROW)
    tables = jax.vmap(one_block)(jax.random.split(key, ROWS // ROW_DEV))
    return tables.reshape(ROWS, PAGES_ROW).astype(jnp.int32)


def draw_kv_cache(key, part):
    key = jax.random.fold_in(key, 14)
    value_key = jax.random.fold_in(key, 0)
    shape_all = (POOL, PAGE, 2 * KVH * HD)
    values = jax.random.normal(value_key, shape_all, jnp.float32)
    return values.astype(jnp.bfloat16)


def plant(values, key, least, largest):
    dims = values.shape
    place = [jax.random.randint(jax.random.fold_in(key, axis), (), 0, dims[axis]) for axis in range(len(dims))]
    values = values.at[tuple(place)].set(least)
    longest = dims.index(max(dims))
    place[longest] = (place[longest] + 1) % dims[longest]
    return values.at[tuple(place)].set(largest)


def block_levels(rng, shape, shards, least, largest):
    factor_of = 1.0
    for dim, blocks in shards:
        draws = jax.random.uniform(jax.random.fold_in(jax.random.fold_in(rng, 6), dim), (blocks,), jnp.float32, least / len(shards), largest / len(shards))
        factor_of = factor_of * jnp.repeat(jnp.exp(draws), shape[dim] // blocks).reshape((-1,) + (1,) * (len(shape) - 1 - dim))
    return factor_of


def noise(rng, extent, width, bound, cuts=(), held_as=jnp.bfloat16):
    entries = jax.random.normal(rng, extent, jnp.float32) * width
    if len(cuts) > 0:
        entries = block_levels(rng, extent, cuts, -0.22, 0.18) * entries
    return jnp.clip(entries, min=-bound, max=bound).astype(held_as)


def setup_inputs(seed: int = 0, part: int = 0) -> dict:
    key_list = jax.random.split(jax.random.key(seed), 13)
    own_keys = jax.random.split(jax.random.fold_in(key_list[12], part), 13)
    return {
        "hidden": noise(own_keys[0], (STEPS, ROWS, D), 1.0, 6.0, ((1, 4), (2, 4))),
        "w_query": noise(key_list[1], (D, HEADS * HD), D ** -0.5, 0.0625, ((1, 4),)),
        "a_codes": noise(key_list[2], (VARIANTS, D, RANK), D ** -0.5, 0.0625, ((0, 4), (1, 4))),
        "a_scales": jnp.clip(jnp.exp(math.log(2.0) - 1.3862944 * jax.random.uniform(key_list[3], (VARIANTS, D), jnp.float32) ** block_levels(key_list[3], (VARIANTS, D), ((0, 4), (1, 4)), -0.2, 0.2)), 0.5, 2.0),
        "b_codes": noise(key_list[4], (VARIANTS, RANK, HEADS * HD), RANK ** -0.5, 0.5, ((0, 4), (2, 4))),
        "b_scales": jnp.clip(jnp.exp(math.log(2.0) - 1.3862944 * jax.random.uniform(key_list[5], (VARIANTS, RANK), jnp.float32) ** block_levels(key_list[5], (VARIANTS, RANK), ((0, 4),), -0.2, 0.2)), 0.5, 2.0),
        "variant_lists": draw_variant_lists(jax.random.fold_in(jax.random.fold_in(key_list[12], part), 71), part),
        "row_pick": plant(jax.random.randint(own_keys[7], (ROWS,), 0, LIST), jax.random.fold_in(own_keys[7], 1), 0, LIST - 1).astype(jnp.int32),
        "lengths": draw_lengths(jax.random.fold_in(jax.random.fold_in(key_list[12], part), 71), part),
        "page_table": draw_page_table(jax.random.fold_in(jax.random.fold_in(key_list[12], part), 71), part),
        "new_kv": noise(own_keys[10], (STEPS, ROWS, 2 * KVH * HD), 1.0, 6.0, ((1, 16),)),
        "kv_cache": draw_kv_cache(jax.random.fold_in(jax.random.fold_in(key_list[12], part), 71), part),
    }


def dequant(code_block, scale_rows):
    return (code_block.astype(jnp.float32) * scale_rows[:, :, None]).astype(jnp.bfloat16)


def group_query(group_rows, group_pick, group_list, w_query, a_codes, a_scales, b_codes, b_scales):
    a_select = dequant(a_codes[group_list], a_scales[group_list])
    b_select = dequant(b_codes[group_list], b_scales[group_list])
    flattened = group_rows.reshape(STEPS * GROUP_ROWS, D)
    base_part = jnp.dot(flattened, w_query, preferred_element_type=jnp.float32)
    onehot = group_pick[:, None] == jnp.arange(LIST, dtype=jnp.int32)[None, :]
    low_all = jnp.einsum('trd,kdc->trkc', group_rows.astype(jnp.float32), a_select.astype(jnp.float32))
    low_sum = jnp.sum(jnp.where(onehot[None, :, :, None], low_all, 0.0), axis=2)
    low_bf = low_sum.astype(jnp.bfloat16)
    spread = jnp.where(onehot[None, :, :, None], low_bf[:, :, None, :], jnp.zeros((), jnp.bfloat16))
    delta_q = jnp.dot(spread.reshape(STEPS * GROUP_ROWS, LIST * RANK), b_select.reshape(LIST * RANK, HEADS * HD), preferred_element_type=jnp.float32)
    return (base_part + delta_q).astype(jnp.bfloat16).reshape(STEPS, GROUP_ROWS, HEADS * HD)


def attend(queries, fresh_kv, row_lengths, row_table, pool_pages):
    row_count = queries.shape[1]
    share_count = HEADS // KVH
    pages_all = jnp.take(pool_pages, row_table.reshape(-1), axis=0).reshape(row_count, CTX, 2, KVH, HD).astype(jnp.float32)
    fresh_all = fresh_kv.reshape(STEPS, row_count, 2, KVH, HD).astype(jnp.float32)
    grouped = queries.reshape(STEPS, row_count, KVH, share_count, HD).astype(jnp.float32)
    inv_scale = HD ** -0.5
    score_old = jnp.einsum('trkgd,rskd->trkgs', grouped, pages_all[:, :, 0]) * inv_scale
    score_new = jnp.einsum('trkgd,urkd->trkgu', grouped, fresh_all[:, :, 0]) * inv_scale
    live_old = jnp.arange(CTX, dtype=jnp.int32)[None, :] < row_lengths[:, None]
    live_new = jnp.arange(STEPS, dtype=jnp.int32)[None, :] <= jnp.arange(STEPS, dtype=jnp.int32)[:, None]
    score_old = jnp.where(live_old[None, :, None, None, :], score_old, -1e30)
    score_new = jnp.where(live_new[:, None, None, None, :], score_new, -1e30)
    row_peak = jnp.maximum(jnp.max(score_old, axis=-1), jnp.max(score_new, axis=-1))
    exp_old = jnp.exp(score_old - row_peak[..., None])
    exp_new = jnp.exp(score_new - row_peak[..., None])
    denominator = jnp.sum(exp_old, axis=-1) + jnp.sum(exp_new, axis=-1)
    weight_old = (exp_old / denominator[..., None]).astype(jnp.bfloat16)
    weight_new = (exp_new / denominator[..., None]).astype(jnp.bfloat16)
    output = jnp.einsum('trkgs,rskd->trkgd', weight_old.astype(jnp.float32), pages_all[:, :, 1])
    output = output + jnp.einsum('trkgu,urkd->trkgd', weight_new.astype(jnp.float32), fresh_all[:, :, 1])
    return output.reshape(STEPS, row_count, HEADS * HD).astype(jnp.bfloat16)


def reference(hidden, w_query, a_codes, a_scales, b_codes, b_scales, variant_lists, row_pick, lengths, page_table, new_kv, kv_cache):
    grouped_rows = hidden.reshape(STEPS, GROUPS, GROUP_ROWS, D).transpose(1, 0, 2, 3)
    grouped_pick = row_pick.reshape(GROUPS, GROUP_ROWS)

    def one_group(items):
        return group_query(items[0], items[1], items[2], w_query, a_codes, a_scales, b_codes, b_scales)

    queries = lax.map(one_group, (grouped_rows, grouped_pick, variant_lists))
    queries = queries.transpose(1, 0, 2, 3).reshape(STEPS, ROWS, HEADS * HD)

    def one_block(block_index):
        first_row = (block_index * ROW_DEV).astype(jnp.int32)
        first_page = (block_index * POOL_DEV).astype(jnp.int32)
        block_query = lax.dynamic_slice_in_dim(queries, first_row, ROW_DEV, 1)
        block_fresh = lax.dynamic_slice_in_dim(new_kv, first_row, ROW_DEV, 1)
        block_lengths = lax.dynamic_slice_in_dim(lengths, first_row, ROW_DEV, 0)
        block_table = lax.dynamic_slice_in_dim(page_table, first_row, ROW_DEV, 0)
        block_pool = lax.dynamic_slice_in_dim(kv_cache, first_page, POOL_DEV, 0)
        return attend(block_query, block_fresh, block_lengths, block_table, block_pool)

    results = lax.map(one_block, jnp.arange(ROWS // ROW_DEV, dtype=jnp.int32))
    return results.transpose(1, 0, 2, 3).reshape(STEPS, ROWS, HEADS * HD)
```

```python
import functools

import jax
import jax.numpy as jnp
from jax import lax
from jax.experimental import pallas as pl
from jax.experimental.pallas import tpu as pltpu
from jax.sharding import PartitionSpec as P

HEADS = 32
KVH = 4
HD = 128
SLOTS = 2
SHARE = HEADS // KVH


def dequant(code_block, scale_rows):
    return (code_block.astype(jnp.float32) * scale_rows[..., None]).astype(jnp.bfloat16)


def attend_kernel(n_steps, len_ref, q_ref, kv_ref, new_ref, out_ref):
    inv_scale = HD ** (-0.5)
    ctx = kv_ref.shape[1]
    n_new = new_ref.shape[1]
    rows, q_rows = q_ref.shape[1], q_ref.shape[2]
    old_pos = lax.broadcasted_iota(jnp.int32, (rows, q_rows, ctx), 2)
    live_old = old_pos < len_ref[...]
    step = lax.broadcasted_iota(jnp.int32, (rows, q_rows, n_new), 1) // SHARE
    new_pos = lax.broadcasted_iota(jnp.int32, (rows, q_rows, n_new), 2)
    live_new = new_pos <= step
    qk = (((2,), (2,)), ((0,), (0,)))
    pv = (((2,), (1,)), ((0,), (0,)))
    for head in range(KVH):
        k_cols = pl.ds(head * HD, HD)
        v_cols = pl.ds((KVH + head) * HD, HD)
        q = q_ref[head]
        s_old = lax.dot_general(q, kv_ref[:, :, k_cols], qk, preferred_element_type=jnp.float32)
        s_new = lax.dot_general(q, new_ref[:, :, k_cols], qk, preferred_element_type=jnp.float32)
        s_old = jnp.where(live_old, s_old * inv_scale, -1e30)
        s_new = jnp.where(live_new, s_new * inv_scale, -1e30)
        peak = jnp.maximum(
            jnp.max(s_old, axis=-1, keepdims=True), jnp.max(s_new, axis=-1, keepdims=True)
        )
        e_old = jnp.exp(s_old - peak)
        e_new = jnp.exp(s_new - peak)
        inv = 1.0 / (
            jnp.sum(e_old, axis=-1, keepdims=True) + jnp.sum(e_new, axis=-1, keepdims=True)
        )
        p_old = (e_old * inv).astype(jnp.bfloat16)
        p_new = (e_new * inv).astype(jnp.bfloat16)
        out = lax.dot_general(p_old, kv_ref[:, :, v_cols], pv, preferred_element_type=jnp.float32)
        out += lax.dot_general(p_new, new_ref[:, :, v_cols], pv, preferred_element_type=jnp.float32)
        out_ref[head] = out.astype(jnp.bfloat16)


def attend(q, pages, fresh, row_lengths, n_steps):
    _, rows, q_rows, _ = q.shape
    ctx, kv_width = pages.shape[1:]
    n_new = fresh.shape[1]
    block = 8 if rows % 8 == 0 else rows
    lens = jnp.broadcast_to(row_lengths[:, None, None], (rows, 1, ctx))
    return pl.pallas_call(
        functools.partial(attend_kernel, n_steps),
        grid=(rows // block,),
        out_shape=jax.ShapeDtypeStruct(q.shape, jnp.bfloat16),
        in_specs=[
            pl.BlockSpec((block, 1, ctx), lambda i: (i, 0, 0)),
            pl.BlockSpec((KVH, block, q_rows, HD), lambda i: (0, i, 0, 0)),
            pl.BlockSpec((block, ctx, kv_width), lambda i: (i, 0, 0)),
            pl.BlockSpec((block, n_new, kv_width), lambda i: (i, 0, 0)),
        ],
        out_specs=pl.BlockSpec((KVH, block, q_rows, HD), lambda i: (0, i, 0, 0)),
        compiler_params=pltpu.CompilerParams(vmem_limit_bytes=32 * 1024 * 1024),
        cost_estimate=pl.CostEstimate(
            flops=4 * KVH * rows * q_rows * HD * ctx,
            bytes_accessed=pages.size * 2 + 2 * q.size * 2,
            transcendentals=KVH * rows * q_rows * ctx,
        ),
    )(lens, q, pages, fresh)


def on_device(
    hidden,
    w_query,
    a_codes,
    a_scales,
    b_codes,
    b_scales,
    variant_lists,
    row_pick,
    lengths,
    page_table,
    new_kv,
    kv_cache,
):
    n_steps, n_rows, width_dev = hidden.shape
    col_count = w_query.shape[1]
    owned, _, rank_size = a_codes.shape
    n_tensor = lax.axis_size("tensor")
    n_dp = lax.axis_size("dp")
    row_dev = lengths.shape[0]
    chunks = 3 if row_dev % 3 == 0 else 1
    row_chunk = row_dev // chunks
    group_index = lax.axis_index("dp")

    by_dev = hidden.reshape(n_steps, n_tensor, row_dev, width_dev)
    gathered = []
    for c in range(chunks):
        part = by_dev[:, :, c * row_chunk : (c + 1) * row_chunk]
        part = part.reshape(n_steps * n_tensor * row_chunk, width_dev)
        gathered.append(lax.all_gather(part, "tensor", axis=1, tiled=True))

    mine = variant_lists // owned == group_index
    rank_in = jnp.cumsum(mine.astype(jnp.int32), axis=1) - 1
    slot_ids = jnp.arange(SLOTS, dtype=jnp.int32)
    hit = mine[:, None, :] & (rank_in[:, None, :] == slot_ids[None, :, None])
    local = jnp.sum(jnp.where(hit, (variant_lists % owned)[:, None, :], 0), axis=2)
    picks = local.reshape(-1)
    a_send = dequant(
        a_codes.at[picks].get(mode="promise_in_bounds"),
        a_scales.at[picks].get(mode="promise_in_bounds"),
    ).reshape(n_dp, SLOTS, width_dev, rank_size)
    b_send = dequant(
        b_codes.at[picks].get(mode="promise_in_bounds"),
        b_scales.at[picks].get(mode="promise_in_bounds"),
    ).reshape(n_dp, SLOTS, rank_size, col_count)
    n_slots = n_dp * SLOTS
    a_select = lax.all_to_all(a_send, "dp", 0, 0, tiled=True).reshape(n_slots, width_dev, rank_size)
    b_select = lax.all_to_all(b_send, "dp", 0, 0, tiled=True).reshape(
        n_slots * rank_size, col_count
    )

    own_list = lax.dynamic_index_in_dim(variant_lists, group_index, 0, keepdims=False)
    owner = own_list // owned
    earlier = jnp.tril(jnp.ones((own_list.shape[0],) * 2, jnp.int32), -1)
    place = jnp.sum((owner[:, None] == owner[None, :]).astype(jnp.int32) * earlier, axis=1)
    slot_of = owner * SLOTS + place
    pick_hot = row_pick[:, None] == jnp.arange(own_list.shape[0], dtype=jnp.int32)[None, :]
    row_slot = jnp.sum(jnp.where(pick_hot, slot_of[None, :], 0), axis=1)
    onehot = row_slot[:, None] == jnp.arange(n_slots, dtype=jnp.int32)[None, :]

    low_all = jnp.einsum("trd,kdc->trkc", hidden, a_select, preferred_element_type=jnp.float32)
    low_part = jnp.sum(jnp.where(onehot[None, :, :, None], low_all, 0.0), axis=2)
    low_bf = lax.psum(low_part, "tensor").astype(jnp.bfloat16)
    spread = jnp.where(onehot[None, :, :, None], low_bf[:, :, None, :], jnp.zeros((), jnp.bfloat16))
    spread = spread.reshape(n_steps, n_tensor, row_dev, n_slots * rank_size)

    fresh = jnp.pad(new_kv.transpose(1, 0, 2), ((0, 0), (0, 16 - n_steps), (0, 0)))
    head_dev = col_count // HD
    outs = []
    for c in range(chunks):
        rows = slice(c * row_chunk, (c + 1) * row_chunk)
        pages = kv_cache.at[page_table[rows].reshape(-1)].get(mode="promise_in_bounds")
        pages = pages.reshape(row_chunk, -1, kv_cache.shape[2])
        base = jnp.dot(gathered[c], w_query, preferred_element_type=jnp.float32)
        delta = jnp.dot(
            spread[:, :, rows].reshape(-1, n_slots * rank_size),
            b_select,
            preferred_element_type=jnp.float32,
        )
        q = (base + delta).astype(jnp.bfloat16)
        q = q.reshape(n_steps, n_tensor, row_chunk, head_dev, HD).transpose(1, 2, 0, 3, 4)
        q = q.reshape(n_tensor, row_chunk, n_steps * head_dev, HD)
        q = lax.all_to_all(q, "tensor", 0, 0, tiled=True)
        q = q.reshape(KVH, n_tensor // KVH, row_chunk, n_steps, head_dev, HD)
        q = q.transpose(0, 2, 3, 1, 4, 5).reshape(KVH, row_chunk, n_steps * SHARE, HD)
        out = attend(q, pages, fresh[rows], lengths[rows], n_steps)
        out = out.reshape(KVH, row_chunk, n_steps, SHARE * HD).transpose(2, 1, 0, 3)
        outs.append(out.reshape(n_steps, row_chunk, HEADS * HD))
    return jnp.concatenate(outs, axis=1)


def solution(mesh):
    placed = (
        P(None, ("replica", "dp"), "tensor"),
        P(None, "tensor"),
        P("dp", "tensor", None),
        P("dp", "tensor"),
        P("dp", None, "tensor"),
        P("dp", None),
        P("replica", None),
        P(("replica", "dp")),
        P(("replica", "dp", "tensor")),
        P(("replica", "dp", "tensor"), None),
        P(None, ("replica", "dp", "tensor"), None),
        P(("replica", "dp", "tensor"), None, None),
    )
    return jax.shard_map(
        on_device,
        mesh=mesh,
        in_specs=placed,
        out_specs=P(None, ("replica", "dp", "tensor"), None),
        check_vma=False,
    )
```

```python
import functools

import jax
import jax.numpy as jnp
from jax import lax
from jax.experimental import pallas as pl
from jax.experimental.pallas import tpu as pltpu
from jax.sharding import PartitionSpec as P

HEADS = 32
KVH = 4
HD = 128
SLOTS = 2
SHARE = HEADS // KVH


def dequant(code_block, scale_rows):
    return (code_block.astype(jnp.float32) * scale_rows[..., None]).astype(jnp.bfloat16)


def attend_kernel(store, len_ref, q_ref, kv_ref, new_ref, *refs):
    inv_scale = HD ** (-0.5)
    ctx = kv_ref.shape[1]
    n_new = new_ref.shape[1]
    rows, q_rows = q_ref.shape[1], q_ref.shape[2]
    old_pos = lax.broadcasted_iota(jnp.int32, (rows, q_rows, ctx), 2)
    live_old = old_pos < len_ref[...]
    step = lax.broadcasted_iota(jnp.int32, (rows, q_rows, n_new), 1) // SHARE
    new_pos = lax.broadcasted_iota(jnp.int32, (rows, q_rows, n_new), 2)
    live_new = new_pos <= step
    qk = (((2,), (2,)), ((0,), (0,)))
    pv = (((2,), (1,)), ((0,), (0,)))
    for head in range(KVH):
        k_cols = pl.ds(head * HD, HD)
        v_cols = pl.ds((KVH + head) * HD, HD)
        q = q_ref[head]
        s_old = lax.dot_general(q, kv_ref[:, :, k_cols], qk, preferred_element_type=jnp.float32)
        s_new = lax.dot_general(q, new_ref[:, :, k_cols], qk, preferred_element_type=jnp.float32)
        s_old = jnp.where(live_old, s_old * inv_scale, -1e30)
        s_new = jnp.where(live_new, s_new * inv_scale, -1e30)
        peak = jnp.maximum(
            jnp.max(s_old, axis=-1, keepdims=True), jnp.max(s_new, axis=-1, keepdims=True)
        )
        e_old = jnp.exp(s_old - peak)
        e_new = jnp.exp(s_new - peak)
        inv = 1.0 / (
            jnp.sum(e_old, axis=-1, keepdims=True) + jnp.sum(e_new, axis=-1, keepdims=True)
        )
        p_old = (e_old * inv).astype(jnp.bfloat16)
        p_new = (e_new * inv).astype(jnp.bfloat16)
        out = lax.dot_general(p_old, kv_ref[:, :, v_cols], pv, preferred_element_type=jnp.float32)
        out += lax.dot_general(p_new, new_ref[:, :, v_cols], pv, preferred_element_type=jnp.float32)
        store(refs[-1], head, out)


def store_heads(out_ref, head, out):
    out_ref[head] = out.astype(jnp.bfloat16)


def store_columns(out_ref, head, out):
    by_query = jnp.swapaxes(out, 0, 1).astype(jnp.bfloat16)
    for step in range(out_ref.shape[0]):
        for share in range(SHARE):
            cols = pl.ds((head * SHARE + share) * HD, HD)
            out_ref[step, :, cols] = by_query[step * SHARE + share]


def attend_into(result, c, q, pages, fresh, row_lengths, row_dev):
    _, rows, q_rows, _ = q.shape
    ctx, kv_width = pages.shape[1:]
    n_steps = q_rows // SHARE
    lens = jnp.broadcast_to(row_lengths[:, None, None], (rows, 1, ctx))
    earlier = [] if result is None else [result]
    return pl.pallas_call(
        functools.partial(attend_kernel, store_columns),
        grid=(1,),
        out_shape=jax.ShapeDtypeStruct((n_steps, row_dev, HEADS * HD), jnp.bfloat16),
        in_specs=[
            pl.BlockSpec((rows, 1, ctx), lambda i: (0, 0, 0)),
            pl.BlockSpec(q.shape, lambda i: (0, 0, 0, 0)),
            pl.BlockSpec(pages.shape, lambda i: (0, 0, 0)),
            pl.BlockSpec(fresh.shape, lambda i: (0, 0, 0)),
        ]
        + [pl.BlockSpec(memory_space=pl.ANY)] * len(earlier),
        out_specs=pl.BlockSpec((n_steps, rows, HEADS * HD), lambda i: (0, c, 0)),
        input_output_aliases={4: 0} if earlier else {},
        compiler_params=pltpu.CompilerParams(vmem_limit_bytes=40 * 1024 * 1024),
        cost_estimate=pl.CostEstimate(
            flops=4 * KVH * rows * q_rows * HD * ctx,
            bytes_accessed=pages.size * 2 + 2 * q.size * 2,
            transcendentals=KVH * rows * q_rows * ctx,
        ),
    )(lens, q, pages, fresh, *earlier)


def attend(q, pages, fresh, row_lengths):
    _, rows, q_rows, _ = q.shape
    ctx, kv_width = pages.shape[1:]
    n_new = fresh.shape[1]
    block = 8 if rows % 8 == 0 else rows
    lens = jnp.broadcast_to(row_lengths[:, None, None], (rows, 1, ctx))
    return pl.pallas_call(
        functools.partial(attend_kernel, store_heads),
        grid=(rows // block,),
        out_shape=jax.ShapeDtypeStruct(q.shape, jnp.bfloat16),
        in_specs=[
            pl.BlockSpec((block, 1, ctx), lambda i: (i, 0, 0)),
            pl.BlockSpec((KVH, block, q_rows, HD), lambda i: (0, i, 0, 0)),
            pl.BlockSpec((block, ctx, kv_width), lambda i: (i, 0, 0)),
            pl.BlockSpec((block, n_new, kv_width), lambda i: (i, 0, 0)),
        ],
        out_specs=pl.BlockSpec((KVH, block, q_rows, HD), lambda i: (0, i, 0, 0)),
        compiler_params=pltpu.CompilerParams(vmem_limit_bytes=32 * 1024 * 1024),
        cost_estimate=pl.CostEstimate(
            flops=4 * KVH * rows * q_rows * HD * ctx,
            bytes_accessed=pages.size * 2 + 2 * q.size * 2,
            transcendentals=KVH * rows * q_rows * ctx,
        ),
    )(lens, q, pages, fresh)


def block_dot(block, w_query, number):
    depth = block.shape[1]
    w_block = lax.dynamic_slice_in_dim(w_query, number * depth, depth, 0)
    return jnp.dot(block, w_block, preferred_element_type=jnp.float32)


def hop_once(from_left, from_right, hop, count):
    right_pairs = [(i, i + 1) for i in range(hop - 1, count - 1)]
    left_pairs = [(i + 1, i) for i in range(count - hop)]
    return (
        lax.ppermute(from_left, "tensor", right_pairs),
        lax.ppermute(from_right, "tensor", left_pairs),
    )


def nth_block(arrived, k, count):
    order = [
        [(h, d) for h in range(1, count) for d in (-1, 1) if 0 <= i + d * h < count]
        for i in range(count)
    ]
    me = lax.axis_index("tensor")
    sources = sorted({order[i][k] for i in range(count)})
    block = arrived[sources[0]]
    number = me + sources[0][0] * sources[0][1]
    for source in sources[1:]:
        here = functools.reduce(
            jnp.logical_or, [me == i for i in range(count) if order[i][k] == source]
        )
        block = jnp.where(here, arrived[source], block)
        number = jnp.where(here, me + source[0] * source[1], number)
    return block, number


def on_device(
    hidden,
    w_query,
    a_codes,
    a_scales,
    b_codes,
    b_scales,
    variant_lists,
    row_pick,
    lengths,
    page_table,
    new_kv,
    kv_cache,
):
    n_steps, n_rows, width_dev = hidden.shape
    col_count = w_query.shape[1]
    owned, _, rank_size = a_codes.shape
    n_tensor = lax.axis_size("tensor")
    n_dp = lax.axis_size("dp")
    row_dev = lengths.shape[0]
    chunks = 3 if row_dev % 3 == 0 else 1
    row_chunk = row_dev // chunks
    group_index = lax.axis_index("dp")

    flat = hidden.reshape(n_steps * n_rows, width_dev)
    relay = 2 < n_tensor <= 8
    arrived = {}
    if relay:
        arrived[(1, -1)], arrived[(1, 1)] = hop_once(flat, flat, 1, n_tensor)

    mine = variant_lists // owned == group_index
    rank_in = jnp.cumsum(mine.astype(jnp.int32), axis=1) - 1
    slot_ids = jnp.arange(SLOTS, dtype=jnp.int32)
    hit = mine[:, None, :] & (rank_in[:, None, :] == slot_ids[None, :, None])
    local = jnp.sum(jnp.where(hit, (variant_lists % owned)[:, None, :], 0), axis=2)
    picks = local.reshape(-1)
    a_send = dequant(
        a_codes.at[picks].get(mode="promise_in_bounds"),
        a_scales.at[picks].get(mode="promise_in_bounds"),
    ).reshape(n_dp, SLOTS, width_dev, rank_size)
    b_send = dequant(
        b_codes.at[picks].get(mode="promise_in_bounds"),
        b_scales.at[picks].get(mode="promise_in_bounds"),
    ).reshape(n_dp, SLOTS, rank_size, col_count)
    n_slots = n_dp * SLOTS
    pages = [
        kv_cache.at[page_table[c * row_chunk : (c + 1) * row_chunk].reshape(-1)]
        .get(mode="promise_in_bounds")
        .reshape(row_chunk, -1, kv_cache.shape[2])
        for c in range(chunks)
    ]
    total = None
    if relay:
        total = block_dot(flat, w_query, lax.axis_index("tensor"))
        far_left, far_right, pages, total, _ = lax.optimization_barrier(
            (arrived[(1, -1)], arrived[(1, 1)], pages, total, b_send)
        )
        arrived[(1, -1)], arrived[(1, 1)] = far_left, far_right
        arrived[(2, -1)], arrived[(2, 1)] = hop_once(far_left, far_right, 2, n_tensor)
    a_select = lax.all_to_all(a_send, "dp", 0, 0, tiled=True).reshape(n_slots, width_dev, rank_size)
    b_select = lax.all_to_all(b_send, "dp", 0, 0, tiled=True).reshape(
        n_slots * rank_size, col_count
    )

    own_list = lax.dynamic_index_in_dim(variant_lists, group_index, 0, keepdims=False)
    owner = own_list // owned
    earlier = jnp.tril(jnp.ones((own_list.shape[0],) * 2, jnp.int32), -1)
    place = jnp.sum((owner[:, None] == owner[None, :]).astype(jnp.int32) * earlier, axis=1)
    slot_of = owner * SLOTS + place
    pick_hot = row_pick[:, None] == jnp.arange(own_list.shape[0], dtype=jnp.int32)[None, :]
    row_slot = jnp.sum(jnp.where(pick_hot, slot_of[None, :], 0), axis=1)
    onehot = row_slot[:, None] == jnp.arange(n_slots, dtype=jnp.int32)[None, :]

    low_all = jnp.einsum("trd,kdc->trkc", hidden, a_select, preferred_element_type=jnp.float32)
    low_part = jnp.sum(jnp.where(onehot[None, :, :, None], low_all, 0.0), axis=2)
    if relay:
        first, number = nth_block(arrived, 0, n_tensor)
        total = total + block_dot(first, w_query, number)
        far_left, far_right = arrived[(2, -1)], arrived[(2, 1)]
        far_left, far_right, total, low_part = lax.optimization_barrier(
            (far_left, far_right, total, low_part)
        )
        arrived[(2, -1)], arrived[(2, 1)] = far_left, far_right
        for hop in range(3, n_tensor):
            far_left, far_right = hop_once(far_left, far_right, hop, n_tensor)
            arrived[(hop, -1)], arrived[(hop, 1)] = far_left, far_right
    low_split = low_part.reshape(n_tensor, -1, rank_size)
    low_mine = jnp.sum(lax.all_to_all(low_split, "tensor", 0, 0), axis=0).astype(jnp.bfloat16)
    low_bf = lax.all_gather(low_mine, "tensor", axis=0, tiled=True)
    low_bf = low_bf.reshape(n_steps, n_rows, rank_size)
    spread = jnp.where(onehot[None, :, :, None], low_bf[:, :, None, :], jnp.zeros((), jnp.bfloat16))
    spread = spread.reshape(n_steps, n_tensor, row_dev, n_slots * rank_size)

    delta = jnp.dot(
        spread.reshape(-1, n_slots * rank_size), b_select, preferred_element_type=jnp.float32
    )
    if relay:
        for k in range(1, n_tensor - 2):
            block, number = nth_block(arrived, k, n_tensor)
            total = total + block_dot(block, w_query, number)
        total = total + delta
        last, last_number = nth_block(arrived, n_tensor - 2, n_tensor)
    else:
        total, last, last_number = delta, lax.all_gather(flat, "tensor", axis=1, tiled=True), 0
    total = total.reshape(n_steps, n_tensor, row_dev, col_count)
    last = last.reshape(n_steps, n_tensor, row_dev, -1)

    fresh = jnp.pad(new_kv.transpose(1, 0, 2), ((0, 0), (0, 16 - n_steps), (0, 0)))
    head_dev = col_count // HD
    outs, result = [], None
    for c in range(chunks):
        rows = slice(c * row_chunk, (c + 1) * row_chunk)
        part = last[:, :, rows].reshape(-1, last.shape[3])
        q = block_dot(part, w_query, last_number) + total[:, :, rows].reshape(-1, col_count)
        q = q.astype(jnp.bfloat16)
        q = q.reshape(n_steps, n_tensor, row_chunk, head_dev, HD).transpose(1, 2, 0, 3, 4)
        q = q.reshape(n_tensor, row_chunk, n_steps * head_dev, HD)
        q = lax.all_to_all(q, "tensor", 0, 0, tiled=True)
        q = q.reshape(KVH, n_tensor // KVH, row_chunk, n_steps, head_dev, HD)
        q = q.transpose(0, 2, 3, 1, 4, 5).reshape(KVH, row_chunk, n_steps * SHARE, HD)
        if row_chunk % 16 == 0:
            result = attend_into(result, c, q, pages[c], fresh[rows], lengths[rows], row_dev)
        else:
            out = attend(q, pages[c], fresh[rows], lengths[rows])
            out = out.reshape(KVH, row_chunk, n_steps, SHARE * HD).transpose(2, 1, 0, 3)
            outs.append(out.reshape(n_steps, row_chunk, HEADS * HD))
    return jnp.concatenate(outs, axis=1) if outs else result


def solution(mesh):
    placed = (
        P(None, ("replica", "dp"), "tensor"),
        P(None, "tensor"),
        P("dp", "tensor", None),
        P("dp", "tensor"),
        P("dp", None, "tensor"),
        P("dp", None),
        P("replica", None),
        P(("replica", "dp")),
        P(("replica", "dp", "tensor")),
        P(("replica", "dp", "tensor"), None),
        P(None, ("replica", "dp", "tensor"), None),
        P(("replica", "dp", "tensor"), None, None),
    )
    return jax.shard_map(
        on_device,
        mesh=mesh,
        in_specs=placed,
        out_specs=P(None, ("replica", "dp", "tensor"), None),
        check_vma=False,
    )
```

```python
import functools

import jax
import jax.numpy as jnp
from jax import lax
from jax.experimental import pallas as pl
from jax.experimental.pallas import tpu as pltpu
from jax.sharding import PartitionSpec as P

HEADS = 32
KVH = 4
HD = 128
SLOTS = 2
SHARE = HEADS // KVH


def dequant(code_block, scale_rows):
    return (code_block.astype(jnp.float32) * scale_rows[..., None]).astype(jnp.bfloat16)


def attend_kernel(store, len_ref, q_ref, kv_ref, new_ref, *refs):
    inv_scale = HD ** (-0.5)
    ctx = kv_ref.shape[1]
    n_new = new_ref.shape[1]
    rows, q_rows = q_ref.shape[1], q_ref.shape[2]
    old_pos = lax.broadcasted_iota(jnp.int32, (rows, q_rows, ctx), 2)
    live_old = old_pos < len_ref[...]
    step = lax.broadcasted_iota(jnp.int32, (rows, q_rows, n_new), 1) // SHARE
    new_pos = lax.broadcasted_iota(jnp.int32, (rows, q_rows, n_new), 2)
    live_new = new_pos <= step
    qk = (((2,), (2,)), ((0,), (0,)))
    pv = (((2,), (1,)), ((0,), (0,)))
    for head in range(KVH):
        k_cols = pl.ds(head * HD, HD)
        v_cols = pl.ds((KVH + head) * HD, HD)
        q = q_ref[head]
        s_old = lax.dot_general(q, kv_ref[:, :, k_cols], qk, preferred_element_type=jnp.float32)
        s_new = lax.dot_general(q, new_ref[:, :, k_cols], qk, preferred_element_type=jnp.float32)
        s_old = jnp.where(live_old, s_old * inv_scale, -1e30)
        s_new = jnp.where(live_new, s_new * inv_scale, -1e30)
        peak = jnp.maximum(
            jnp.max(s_old, axis=-1, keepdims=True), jnp.max(s_new, axis=-1, keepdims=True)
        )
        e_old = jnp.exp(s_old - peak)
        e_new = jnp.exp(s_new - peak)
        inv = 1.0 / (
            jnp.sum(e_old, axis=-1, keepdims=True) + jnp.sum(e_new, axis=-1, keepdims=True)
        )
        p_old = (e_old * inv).astype(jnp.bfloat16)
        p_new = (e_new * inv).astype(jnp.bfloat16)
        out = lax.dot_general(p_old, kv_ref[:, :, v_cols], pv, preferred_element_type=jnp.float32)
        out += lax.dot_general(p_new, new_ref[:, :, v_cols], pv, preferred_element_type=jnp.float32)
        store(refs[-1], head, out)


def store_heads(out_ref, head, out):
    out_ref[head] = out.astype(jnp.bfloat16)


def store_columns(out_ref, head, out):
    by_query = jnp.swapaxes(out, 0, 1).astype(jnp.bfloat16)
    for step in range(out_ref.shape[0]):
        for share in range(SHARE):
            cols = pl.ds((head * SHARE + share) * HD, HD)
            out_ref[step, :, cols] = by_query[step * SHARE + share]


def attend_into(result, first_row, q, pages, fresh, row_lengths, row_dev):
    _, rows, q_rows, _ = q.shape
    ctx, kv_width = pages.shape[1:]
    n_steps = q_rows // SHARE
    lens = jnp.broadcast_to(row_lengths[:, None, None], (rows, 1, ctx))
    earlier = [] if result is None else [result]
    block = 16
    return pl.pallas_call(
        functools.partial(attend_kernel, store_columns),
        grid=(rows // block,),
        out_shape=jax.ShapeDtypeStruct((n_steps, row_dev, HEADS * HD), jnp.bfloat16),
        in_specs=[
            pl.BlockSpec((block, 1, ctx), lambda i: (i, 0, 0)),
            pl.BlockSpec((KVH, block, q_rows, HD), lambda i: (0, i, 0, 0)),
            pl.BlockSpec((block, ctx, kv_width), lambda i: (i, 0, 0)),
            pl.BlockSpec((block, fresh.shape[1], kv_width), lambda i: (i, 0, 0)),
        ]
        + [pl.BlockSpec(memory_space=pl.ANY)] * len(earlier),
        out_specs=pl.BlockSpec(
            (n_steps, block, HEADS * HD), lambda i: (0, first_row // block + i, 0)
        ),
        input_output_aliases={4: 0} if earlier else {},
        compiler_params=pltpu.CompilerParams(vmem_limit_bytes=40 * 1024 * 1024),
        cost_estimate=pl.CostEstimate(
            flops=4 * KVH * rows * q_rows * HD * ctx,
            bytes_accessed=pages.size * 2 + 2 * q.size * 2,
            transcendentals=KVH * rows * q_rows * ctx,
        ),
    )(lens, q, pages, fresh, *earlier)


def attend(q, pages, fresh, row_lengths):
    _, rows, q_rows, _ = q.shape
    ctx, kv_width = pages.shape[1:]
    n_new = fresh.shape[1]
    block = 8 if rows % 8 == 0 else rows
    lens = jnp.broadcast_to(row_lengths[:, None, None], (rows, 1, ctx))
    return pl.pallas_call(
        functools.partial(attend_kernel, store_heads),
        grid=(rows // block,),
        out_shape=jax.ShapeDtypeStruct(q.shape, jnp.bfloat16),
        in_specs=[
            pl.BlockSpec((block, 1, ctx), lambda i: (i, 0, 0)),
            pl.BlockSpec((KVH, block, q_rows, HD), lambda i: (0, i, 0, 0)),
            pl.BlockSpec((block, ctx, kv_width), lambda i: (i, 0, 0)),
            pl.BlockSpec((block, n_new, kv_width), lambda i: (i, 0, 0)),
        ],
        out_specs=pl.BlockSpec((KVH, block, q_rows, HD), lambda i: (0, i, 0, 0)),
        compiler_params=pltpu.CompilerParams(vmem_limit_bytes=32 * 1024 * 1024),
        cost_estimate=pl.CostEstimate(
            flops=4 * KVH * rows * q_rows * HD * ctx,
            bytes_accessed=pages.size * 2 + 2 * q.size * 2,
            transcendentals=KVH * rows * q_rows * ctx,
        ),
    )(lens, q, pages, fresh)


def block_dot(block, w_query, number):
    depth = block.shape[1]
    w_block = lax.dynamic_slice_in_dim(w_query, number * depth, depth, 0)
    return jnp.dot(block, w_block, preferred_element_type=jnp.float32)


def hop_once(from_left, from_right, hop, count):
    right_pairs = [(i, i + 1) for i in range(hop - 1, count - 1)]
    left_pairs = [(i + 1, i) for i in range(count - hop)]
    return (
        lax.ppermute(from_left, "tensor", right_pairs),
        lax.ppermute(from_right, "tensor", left_pairs),
    )


def nth_block(arrived, k, count):
    order = [
        [(h, d) for h in range(1, count) for d in (-1, 1) if 0 <= i + d * h < count]
        for i in range(count)
    ]
    me = lax.axis_index("tensor")
    sources = sorted({order[i][k] for i in range(count)})
    block = arrived[sources[0]]
    number = me + sources[0][0] * sources[0][1]
    for source in sources[1:]:
        here = functools.reduce(
            jnp.logical_or, [me == i for i in range(count) if order[i][k] == source]
        )
        block = jnp.where(here, arrived[source], block)
        number = jnp.where(here, me + source[0] * source[1], number)
    return block, number


def on_device(
    hidden,
    w_query,
    a_codes,
    a_scales,
    b_codes,
    b_scales,
    variant_lists,
    row_pick,
    lengths,
    page_table,
    new_kv,
    kv_cache,
):
    n_steps, n_rows, width_dev = hidden.shape
    col_count = w_query.shape[1]
    owned, _, rank_size = a_codes.shape
    n_tensor = lax.axis_size("tensor")
    n_dp = lax.axis_size("dp")
    row_dev = lengths.shape[0]
    third = row_dev // 3
    spans = [(i * third, third) for i in range(3)] if row_dev % 3 == 0 else [(0, row_dev)]
    group_index = lax.axis_index("dp")

    flat = hidden.reshape(n_steps * n_rows, width_dev)
    fresh = jnp.pad(new_kv.transpose(1, 0, 2), ((0, 0), (0, 16 - n_steps), (0, 0)))
    fresh = [fresh[start : start + size] for start, size in spans]
    relay = n_tensor == 4
    arrived = {}
    if relay:
        arrived[(1, -1)], arrived[(1, 1)] = hop_once(flat, flat, 1, n_tensor)

    mine = variant_lists // owned == group_index
    rank_in = jnp.cumsum(mine.astype(jnp.int32), axis=1) - 1
    slot_ids = jnp.arange(SLOTS, dtype=jnp.int32)
    hit = mine[:, None, :] & (rank_in[:, None, :] == slot_ids[None, :, None])
    local = jnp.sum(jnp.where(hit, (variant_lists % owned)[:, None, :], 0), axis=2)
    picks = local.reshape(-1)
    a_send = dequant(
        a_codes.at[picks].get(mode="promise_in_bounds"),
        a_scales.at[picks].get(mode="promise_in_bounds"),
    ).reshape(n_dp, SLOTS, width_dev, rank_size)
    b_send = dequant(
        b_codes.at[picks].get(mode="promise_in_bounds"),
        b_scales.at[picks].get(mode="promise_in_bounds"),
    ).reshape(n_dp, SLOTS, rank_size, col_count)
    n_slots = n_dp * SLOTS
    pages = [
        kv_cache.at[page_table[start : start + size].reshape(-1)]
        .get(mode="promise_in_bounds")
        .reshape(size, -1, kv_cache.shape[2])
        for start, size in spans
    ]
    total = None
    if relay:
        total = block_dot(flat, w_query, lax.axis_index("tensor"))
        far_left, far_right, pages[0], total, _ = lax.optimization_barrier(
            (arrived[(1, -1)], arrived[(1, 1)], pages[0], total, b_send)
        )
        arrived[(1, -1)], arrived[(1, 1)] = far_left, far_right
        arrived[(2, -1)], arrived[(2, 1)] = hop_once(far_left, far_right, 2, n_tensor)
    a_select = lax.all_to_all(a_send, "dp", 0, 0, tiled=True).reshape(n_slots, width_dev, rank_size)
    b_select = lax.all_to_all(b_send, "dp", 0, 0, tiled=True).reshape(
        n_slots * rank_size, col_count
    )

    own_list = lax.dynamic_index_in_dim(variant_lists, group_index, 0, keepdims=False)
    owner = own_list // owned
    earlier = jnp.tril(jnp.ones((own_list.shape[0],) * 2, jnp.int32), -1)
    place = jnp.sum((owner[:, None] == owner[None, :]).astype(jnp.int32) * earlier, axis=1)
    slot_of = owner * SLOTS + place
    pick_hot = row_pick[:, None] == jnp.arange(own_list.shape[0], dtype=jnp.int32)[None, :]
    row_slot = jnp.sum(jnp.where(pick_hot, slot_of[None, :], 0), axis=1)
    onehot = row_slot[:, None] == jnp.arange(n_slots, dtype=jnp.int32)[None, :]

    low_all = jnp.einsum("trd,kdc->trkc", hidden, a_select, preferred_element_type=jnp.float32)
    low_part = jnp.sum(jnp.where(onehot[None, :, :, None], low_all, 0.0), axis=2)
    if relay:
        first, number = nth_block(arrived, 0, n_tensor)
        total = total + block_dot(first, w_query, number)
        fresh, pages[1:], total, low_part, far_left, far_right = lax.optimization_barrier(
            (fresh, pages[1:], total, low_part, arrived[(2, -1)], arrived[(2, 1)])
        )
        arrived[(2, -1)], arrived[(2, 1)] = far_left, far_right
        me = lax.axis_index("tensor")
        middle = jnp.where(
            me == 1, far_right, jnp.where(me == 2, far_left, jnp.zeros((), far_left.dtype))
        )
        last = lax.ppermute(middle, "tensor", [(2, 3), (1, 0)])
        last_number = jnp.where(me < 2, 3, 0)
    low_split = low_part.reshape(n_tensor, -1, rank_size)
    low_mine = jnp.sum(lax.all_to_all(low_split, "tensor", 0, 0), axis=0).astype(jnp.bfloat16)
    if relay:
        for k in range(1, n_tensor - 2):
            block, number = nth_block(arrived, k, n_tensor)
            total = total + block_dot(block, w_query, number)
        total = total + block_dot(middle, w_query, last_number)
    low_bf = lax.all_gather(low_mine, "tensor", axis=0, tiled=True)
    low_bf = low_bf.reshape(n_steps, n_rows, rank_size)
    if relay:
        low_bf, total = lax.optimization_barrier((low_bf, total))
    spread = jnp.where(onehot[None, :, :, None], low_bf[:, :, None, :], jnp.zeros((), jnp.bfloat16))
    spread = spread.reshape(n_steps, n_tensor, row_dev, n_slots * rank_size)

    delta = jnp.dot(
        spread.reshape(-1, n_slots * rank_size), b_select, preferred_element_type=jnp.float32
    )
    if relay:
        total = total + delta
    else:
        total, last, last_number = delta, lax.all_gather(flat, "tensor", axis=1, tiled=True), 0
    total = total.reshape(n_steps, n_tensor, row_dev, col_count)
    last = last.reshape(n_steps, n_tensor, row_dev, -1)

    head_dev = col_count // HD
    outs, result = [], None
    for c, (first_row, row_chunk) in enumerate(spans):
        rows = slice(first_row, first_row + row_chunk)
        part = last[:, :, rows].reshape(-1, last.shape[3])
        q = block_dot(part, w_query, last_number) + total[:, :, rows].reshape(-1, col_count)
        q = q.astype(jnp.bfloat16)
        q = q.reshape(n_steps, n_tensor, row_chunk, head_dev, HD).transpose(1, 2, 0, 3, 4)
        q = q.reshape(n_tensor, row_chunk, n_steps * head_dev, HD)
        q = lax.all_to_all(q, "tensor", 0, 0, tiled=True)
        q = q.reshape(KVH, n_tensor // KVH, row_chunk, n_steps, head_dev, HD)
        q = q.transpose(0, 2, 3, 1, 4, 5).reshape(KVH, row_chunk, n_steps * SHARE, HD)
        if all(size % 16 == 0 for _, size in spans):
            result = attend_into(result, first_row, q, pages[c], fresh[c], lengths[rows], row_dev)
        else:
            out = attend(q, pages[c], fresh[c], lengths[rows])
            out = out.reshape(KVH, row_chunk, n_steps, SHARE * HD).transpose(2, 1, 0, 3)
            outs.append(out.reshape(n_steps, row_chunk, HEADS * HD))
    return jnp.concatenate(outs, axis=1) if outs else result


def solution(mesh):
    placed = (
        P(None, ("replica", "dp"), "tensor"),
        P(None, "tensor"),
        P("dp", "tensor", None),
        P("dp", "tensor"),
        P("dp", None, "tensor"),
        P("dp", None),
        P("replica", None),
        P(("replica", "dp")),
        P(("replica", "dp", "tensor")),
        P(("replica", "dp", "tensor"), None),
        P(None, ("replica", "dp", "tensor"), None),
        P(("replica", "dp", "tensor"), None, None),
    )
    return jax.shard_map(
        on_device,
        mesh=mesh,
        in_specs=placed,
        out_specs=P(None, ("replica", "dp", "tensor"), None),
        check_vma=False,
    )
```
